256 devices in a mesh: row: 16 (over y_hi, x, core), col: 16 (over y_lo, z).
Axes of the slice: x: 4, y: 4 (y_hi: 2, y_lo: 2; y = y_hi * 2 + y_lo), z: 8, core: 2. Of those that a mesh axis runs over, the one named last changes fastest.
Arguments:
- basis_codes: bfloat16 [7168, 7168], P('row', 'col'), may hold values from -4 to 4
- code_scales: float32 [56, 7168], P(None, 'col'), may hold values from 0.006 to 0.06
- new_basis: float32 [7168, 7168], P('col', 'row'), may hold values from -6 to 6
- moment: float32 [7168, 9216], P('row', 'col'), may hold values from -0.0625 to 0.0625
Outputs:
- margin: float32 [7168, 7168], P('row', 'col')
- rotated_moment: float32 [7168, 9216], P('row', 'col')
The draws below stay inside these ranges and needn't reach their ends.
All inputs are finite; a program needn't handle non-finite values.
Results may differ from the reference program's by a relative error of at most 0.0057.
Values may be sent and summed in bfloat16 or wider, within the bound.
No kernel may reach another device: no remote copies, remote signals or barrier semaphores. Data moves between devices by JAX's collectives and lax.ppermute only.
A program may use at most 128 MiB of HBM per device.

```python
import math
import jax
import jax.numpy as jnp
from jax import lax

D = 7168
F = 9216
GROUPS = 56


def draw_basis_codes(key, part):
    key = jax.random.fold_in(key, 11)
    values = jnp.clip(jax.random.normal(key, (D, D), jnp.float32), -4.0, 4.0)
    return values.astype(jnp.bfloat16)


def block_levels(own_key, dims, pieces, smallest, high):
    gain = 1.0
    for dim, parts in pieces:
        steps = jax.random.uniform(jax.random.fold_in(jax.random.fold_in(own_key, 6), dim), (parts,), jnp.float32, smallest / len(pieces), high / len(pieces))
        gain = gain * jnp.repeat(jnp.exp(steps), dims[dim] // parts).reshape((-1,) + (1,) * (len(dims) - 1 - dim))
    return gain


def centred(own_key, shape, scale, most, pieces=(), held_as=jnp.bfloat16):
    entries = jax.random.normal(own_key, shape, jnp.float32) * scale
    if len(pieces) > 0:
        entries = block_levels(own_key, shape, pieces, -0.22, 0.18) * entries
    return jnp.clip(entries, min=-most, max=most).astype(held_as)


def setup_inputs(seed: int = 0) -> dict:
    keys = jax.random.split(jax.random.key(seed), 5)
    return {
        "basis_codes": draw_basis_codes(jax.random.fold_in(keys[4], 71), 0),
        "code_scales": jnp.clip(jnp.exp(math.log(0.06) - 2.3025851 * jax.random.uniform(keys[1], (GROUPS, D), jnp.float32) ** block_levels(keys[1], (GROUPS, D), ((1, 16),), -0.2, 0.2)), 0.006, 0.06),
        "new_basis": centred(keys[2], (D, D), 1.0, 6.0, ((0, 16), (1, 16)), jnp.float32),
        "moment": centred(keys[3], (D, F), D ** -0.5, 0.0625, ((0, 16), (1, 16)), jnp.float32),
    }


def reference(basis_codes, code_scales, new_basis, moment):
    table = jnp.repeat(code_scales, 128, axis=0)
    old_basis = (basis_codes.astype(jnp.float32) * table).astype(jnp.bfloat16)
    new_rounded = new_basis.astype(jnp.bfloat16)
    margin = lax.dot_general(new_rounded, old_basis, (((0,), (0,)), ((), ())), preferred_element_type=jnp.float32)
    margin_rounded = margin.astype(jnp.bfloat16)
    rotated_moment = jnp.dot(margin_rounded, moment.astype(jnp.bfloat16), preferred_element_type=jnp.float32)
    return margin, rotated_moment
```

```python
import functools

import jax
import jax.numpy as jnp
from jax import lax
from jax.experimental import pallas as pl
from jax.experimental.pallas import tpu as pltpu
from jax.sharding import PartitionSpec as P

AXES = ("row", "col")
B = 448
HALF = B // 2
QUARTER = B // 4


def dev(x, yh, yl, z, c):
    return (yh * 8 + x * 2 + c) * 16 + yl * 8 + z


def everyone():
    return [
        (x, yh, yl, z, c)
        for x in range(4)
        for yh in range(2)
        for yl in range(2)
        for z in range(8)
        for c in range(2)
    ]


def perm_of(move):
    return [(dev(*d), dev(*move(*d))) for d in everyone()]


Z_UP = perm_of(lambda x, yh, yl, z, c: (x, yh, yl, (z + 1) % 8, c))
Z_DOWN = perm_of(lambda x, yh, yl, z, c: (x, yh, yl, (z - 1) % 8, c))
X_UP = perm_of(lambda x, yh, yl, z, c: ((x + 1) % 4, yh, yl, z, c))
X_DOWN = perm_of(lambda x, yh, yl, z, c: ((x - 1) % 4, yh, yl, z, c))
CORE = perm_of(lambda x, yh, yl, z, c: (x, yh, yl, z, 1 - c))
YL = perm_of(lambda x, yh, yl, z, c: (x, yh, 1 - yl, z, c))
Y_SWAP_TO = {0: 3, 3: 0, 1: 2, 2: 1}
Y_OUT_TO = {1: 0, 2: 3, 0: 1, 3: 2}


def y_perm(to, senders):
    def move(x, yh, yl, z, c):
        y = to[yh * 2 + yl]
        return (x, y // 2, y % 2, z, c)

    return [
        (dev(*d), dev(*move(*d))) for d in everyone() if d[1] * 2 + d[2] in senders
    ]


Y_SWAP = y_perm(Y_SWAP_TO, (0, 1, 2, 3))
Y_OUT = y_perm(Y_OUT_TO, (1, 2))
Y_RELAY = y_perm(Y_OUT_TO, (0, 3))


def send(v, perm):
    return lax.ppermute(v, AXES, perm)


def rounds(*values):
    return lax.optimization_barrier(values)


def call(kernel, shapes, operands, flops=0, space=pltpu.VMEM, scratch=(), grant=12):
    shapes = [jax.ShapeDtypeStruct(shape, kind) for shape, kind in shapes]
    moved = sum(v.size * v.dtype.itemsize for v in [*operands, *shapes])
    return pl.pallas_call(
        kernel,
        out_shape=shapes,
        in_specs=[pl.BlockSpec(memory_space=space)] * len(operands),
        out_specs=[pl.BlockSpec(memory_space=pltpu.VMEM)] * len(shapes),
        scratch_shapes=scratch,
        compiler_params=pltpu.CompilerParams(vmem_limit_bytes=grant * 1024 * 1024),
        cost_estimate=pl.CostEstimate(
            flops=flops, bytes_accessed=moved, transcendentals=0
        ),
    )(*operands)


def packed(v):
    n = v.shape[0] // 2
    return jnp.concatenate([v[:n], v[n:]], axis=1)


def unpacked(v):
    m = v.shape[1] // 2
    return jnp.concatenate([v[:, :m], v[:, m:]], axis=0)


def bases_kernel(new_hbm, codes_hbm, scales_hbm, new_out, old_out, new_ref, codes_ref, scales_ref, sems):
    copies = [
        pltpu.make_async_copy(source, target, sems.at[n])
        for n, (source, target) in enumerate(
            ((new_hbm, new_ref), (codes_hbm, codes_ref), (scales_hbm, scales_ref))
        )
    ]
    for copy in copies:
        copy.start()
    copies[0].wait()
    new_out[...] = packed(new_ref[...].T.astype(jnp.bfloat16))
    r = lax.axis_index("row")
    odd = lax.rem(r, 2) == 1
    first = lax.div(r * 7, 2)
    copies[1].wait()
    copies[2].wait()
    for k in range(7):
        rows = slice(k * 64, (k + 1) * 64)
        group = first + jnp.where(odd, (k + 1) // 2, k // 2)
        scale = scales_ref[pl.ds(group, 1), :]
        part = (codes_ref[rows].astype(jnp.float32) * scale).astype(jnp.bfloat16)
        if k < 3:
            old_out[rows, :B] = part
        elif k == 3:
            old_out[k * 64 :, :B] = part[:32]
            old_out[:32, B:] = part[32:]
        else:
            old_out[k * 64 - HALF : (k + 1) * 64 - HALF, B:] = part


OLD_ORDER = ((0, 0), (0, 1), (1, 0), (1, 1), (3, 0), (3, 1), (2, 0), (2, 1))


def margin_kernel(slot, a_ref, *refs):
    b_refs, outs, (a_buf, b_buf, sems) = refs[:8], refs[8:10], refs[10:]
    row = lax.axis_index("row")
    x = lax.div(lax.rem(row, 8), 2)
    c = lax.rem(row, 2)
    copies = []
    for n, (t, u) in enumerate(OLD_ORDER):
        kb = lax.rem(x + t, 4) * 2 + (c if u == 0 else 1 - c)
        copies.append(
            (
                pltpu.make_async_copy(a_ref.at[kb], a_buf.at[n], sems.at[0, n]),
                pltpu.make_async_copy(b_refs[n], b_buf.at[n], sems.at[1, n]),
            )
        )
    for pair in copies:
        for priority, copy in enumerate(pair):
            copy.start(priority=priority)
    total = None
    for n, pair in enumerate(copies):
        for copy in pair:
            copy.wait()
        term = jnp.dot(
            unpacked(a_buf[n]), unpacked(b_buf[n]), preferred_element_type=jnp.float32
        )
        total = term if total is None else total + term
    for half, out_ref in enumerate(outs):
        part = total[half * HALF : (half + 1) * HALF]
        out_ref[...] = packed(part.astype(jnp.bfloat16)) if slot == 0 else part


MARGIN_SCRATCH = (
    pltpu.VMEM((8, HALF, 2 * B), jnp.bfloat16),
    pltpu.VMEM((8, HALF, 2 * B), jnp.bfloat16),
    pltpu.SemaphoreType.DMA((2, 8)),
)


def margin_sum_kernel(keep_ref, other_ref, margin_ref, out_ref):
    margin = keep_ref[...] + unpacked(other_ref[...]).astype(jnp.float32)
    margin_ref[...] = margin
    out_ref[...] = packed(margin.astype(jnp.bfloat16))


def moment_kernel(moment_ref, out_ref):
    out_ref[...] = packed(moment_ref[...].astype(jnp.bfloat16))


def moment_pair_kernel(own_ref, in_ref, out_ref, relay_ref, pair_ref):
    edge = lax.div(lax.axis_index("col"), 8) == lax.div(lax.axis_index("row"), 8)
    width = pair_ref.shape[1] // 2

    @pl.when(edge)
    def _():
        pair_ref[:, :width] = unpacked(out_ref[...])
        pair_ref[:, width:] = unpacked(own_ref[...])

    @pl.when(jnp.logical_not(edge))
    def _():
        pair_ref[:, :width] = unpacked(in_ref[...])
        pair_ref[:, width:] = unpacked(relay_ref[...])


def rotate_kernel(slot, b_ref, *refs):
    a_refs, out_ref = refs[:8], refs[8]
    z = lax.rem(lax.axis_index("col"), 8)
    width = b_ref.shape[2] // 2
    total = None
    for s in range(8):
        term = jnp.dot(
            unpacked(a_refs[s][...]),
            b_ref[lax.rem(z + s, 8), :, slot * width : (slot + 1) * width],
            preferred_element_type=jnp.float32,
        )
        total = term if total is None else total + term
    out_ref[...] = packed(total.astype(jnp.bfloat16)) if slot == 0 else total


def rotate_sum_kernel(keep_a, other_a, keep_b, other_b, out_ref):
    out_ref[:HALF] = keep_a[...] + unpacked(other_a[...]).astype(jnp.float32)
    out_ref[HALF:] = keep_b[...] + unpacked(other_b[...]).astype(jnp.float32)


def z_gather(top, bottom, margin):
    rings = []
    ups, downs = ([top], [bottom]), ([top], [bottom])
    for step in range(4):
        for i in range(2):
            if step < 3 or i == 0:
                ups[i].append(send(ups[i][-1], Z_UP))
            if step < 3 or i == 1:
                downs[i].append(send(downs[i][-1], Z_DOWN))
        if step == 1:
            ups[0][-1], margin = rounds(ups[0][-1], margin)
    for i in range(2):
        u, d = ups[i], downs[i]
        far = u[4] if i == 0 else d[4]
        rings.append([u[0], d[1], d[2], d[3], far, u[3], u[2], u[1]])
    return rings, margin


def body(basis_codes, code_scales, new_basis, moment):
    width = moment.shape[1]
    bf16, f32 = jnp.bfloat16, jnp.float32
    new_t, o = call(
        bases_kernel,
        [((HALF, 2 * B), bf16)] * 2,
        [new_basis, basis_codes, code_scales],
        space=pl.ANY,
        scratch=(
            pltpu.VMEM((B, B), f32),
            pltpu.VMEM((B, B), bf16),
            pltpu.VMEM(code_scales.shape, f32),
            pltpu.SemaphoreType.DMA((3,)),
        ),
        grant=60,
    )
    groups8 = [list(range(8)), list(range(8, 16))]
    a_all = lax.all_gather(new_t, "col", axis_index_groups=groups8)
    edge = lax.axis_index("col") // 8 == lax.axis_index("row") // 8

    o_in, o_out = send(o, Y_SWAP), send(o, Y_OUT)
    o_in, o_out, moment = rounds(o_in, o_out, moment)
    o0 = jnp.where(edge, o_out, o_in)
    o_relay, o0b, o0a = send(o_in, Y_RELAY), send(o0, X_UP), send(o0, X_DOWN)
    (m,) = call(moment_kernel, [((HALF, 2 * width), bf16)], [moment])
    m_in, m_out = send(m, Y_SWAP), send(m, Y_OUT)
    o_relay, o0b, o0a = rounds(o_relay, o0b, o0a)
    o1 = jnp.where(edge, o, o_relay)
    o1b, o1a = send(o1, X_UP), send(o1, X_DOWN)
    m_in, o0a_, o0b_ = rounds(m_in, o0a, o0b)
    m_out, o0a_, o0b_ = rounds(m_out, o0a_, o0b_)
    o0ac, o0bc, m_relay = send(o0a_, CORE), send(o0b_, CORE), send(m_in, Y_RELAY)
    o1b, o1a, o0b, o0, o0ac, o0bc = rounds(o1b, o1a, o0b, o0, o0ac, o0bc)
    o0f, o1f = send(o0b, X_UP), send(o1a, X_DOWN)
    o0c = send(o0, CORE)
    (m01,) = call(moment_pair_kernel, [((B, 2 * width), bf16)], [m, m_in, m_out, m_relay])
    o0f, o1f, o0c, m01 = rounds(o0f, o1f, o0c, m01)
    m_all = lax.all_gather(m01, "row", axis_index_groups=groups8)
    o0f, o1f, a_all = rounds(o0f, o1f, a_all)
    o0fc, o1fc = send(o0f, CORE), send(o1f, CORE)
    o0fc, *near_1 = rounds(o0fc, o1, o1a, o1b)
    o1c, o1ac, o1bc = (send(v, CORE) for v in near_1)

    others = call(
        functools.partial(margin_kernel, 0),
        [((QUARTER, 2 * B), bf16)] * 2,
        [a_all, o0, o0c, o0a, o0ac, o0b, o0bc, o0f, o0fc],
        flops=2 * B * B * 8 * B,
        space=pl.ANY,
        scratch=MARGIN_SCRATCH,
        grant=58,
    )
    keeps = call(
        functools.partial(margin_kernel, 1),
        [((HALF, B), f32)] * 2,
        [a_all, o1, o1c, o1a, o1ac, o1b, o1bc, o1f, o1fc],
        flops=2 * B * B * 8 * B,
        space=pl.ANY,
        scratch=MARGIN_SCRATCH,
        grant=58,
    )
    margins, halves = [], []
    for keep, other in zip(keeps, others):
        margin, half = call(
            margin_sum_kernel,
            [((HALF, B), f32), ((QUARTER, 2 * B), bf16)],
            [keep, send(other, YL)],
        )
        margins.append(margin)
        halves.append(half)
    margin = jnp.stack(margins).reshape(B, B)
    rings, margin = z_gather(*halves, margin)
    parts = []
    for slot in range(2):
        for half, ring in enumerate(rings):
            shape = ((QUARTER, 2 * width), bf16) if slot == 0 else ((HALF, width), f32)
            (out,) = call(
                functools.partial(rotate_kernel, slot),
                [shape],
                [m_all, *ring],
                flops=2 * HALF * B * 8 * width,
            )
            parts.append(send(out, YL) if slot == 0 else out)
    other_a, other_b, keep_a, keep_b = parts
    (rotated,) = call(
        rotate_sum_kernel, [((B, width), f32)], [keep_a, other_a, keep_b, other_b]
    )
    return margin, rotated


def solution(mesh):
    return jax.shard_map(
        body,
        mesh=mesh,
        in_specs=(P("row", "col"), P(None, "col"), P("col", "row"), P("row", "col")),
        out_specs=(P("row", "col"), P("row", "col")),
        check_vma=False,
    )
```

```python
import functools

import jax
import jax.numpy as jnp
from jax import lax
from jax.experimental import pallas as pl
from jax.experimental.pallas import tpu as pltpu
from jax.sharding import PartitionSpec as P

AXES = ("row", "col")
B = 448
HALF = B // 2
QUARTER = B // 4


def dev(x, yh, yl, z, c):
    return (yh * 8 + x * 2 + c) * 16 + yl * 8 + z


def everyone():
    return [
        (x, yh, yl, z, c)
        for x in range(4)
        for yh in range(2)
        for yl in range(2)
        for z in range(8)
        for c in range(2)
    ]


def perm_of(move):
    return [(dev(*d), dev(*move(*d))) for d in everyone()]


Z_UP = perm_of(lambda x, yh, yl, z, c: (x, yh, yl, (z + 1) % 8, c))
Z_DOWN = perm_of(lambda x, yh, yl, z, c: (x, yh, yl, (z - 1) % 8, c))
X_UP = perm_of(lambda x, yh, yl, z, c: ((x + 1) % 4, yh, yl, z, c))
X_DOWN = perm_of(lambda x, yh, yl, z, c: ((x - 1) % 4, yh, yl, z, c))
CORE = perm_of(lambda x, yh, yl, z, c: (x, yh, yl, z, 1 - c))
YL = perm_of(lambda x, yh, yl, z, c: (x, yh, 1 - yl, z, c))
Y_SWAP_TO = {0: 3, 3: 0, 1: 2, 2: 1}
Y_OUT_TO = {1: 0, 2: 3, 0: 1, 3: 2}


def y_perm(to, senders):
    def move(x, yh, yl, z, c):
        y = to[yh * 2 + yl]
        return (x, y // 2, y % 2, z, c)

    return [
        (dev(*d), dev(*move(*d))) for d in everyone() if d[1] * 2 + d[2] in senders
    ]


Y_SWAP = y_perm(Y_SWAP_TO, (0, 1, 2, 3))
Y_OUT = y_perm(Y_OUT_TO, (1, 2))
Y_RELAY = y_perm(Y_OUT_TO, (0, 3))


def send(v, perm):
    return lax.ppermute(v, AXES, perm)


def rounds(*values):
    return lax.optimization_barrier(values)


def call(kernel, shapes, operands, flops=0, space=pltpu.VMEM, scratch=(), grant=12):
    shapes = [jax.ShapeDtypeStruct(shape, kind) for shape, kind in shapes]
    moved = sum(v.size * v.dtype.itemsize for v in [*operands, *shapes])
    return pl.pallas_call(
        kernel,
        out_shape=shapes,
        in_specs=[pl.BlockSpec(memory_space=space)] * len(operands),
        out_specs=[pl.BlockSpec(memory_space=pltpu.VMEM)] * len(shapes),
        scratch_shapes=scratch,
        compiler_params=pltpu.CompilerParams(vmem_limit_bytes=grant * 1024 * 1024),
        cost_estimate=pl.CostEstimate(
            flops=flops, bytes_accessed=moved, transcendentals=0
        ),
    )(*operands)


def packed(v):
    n = v.shape[0] // 2
    return jnp.concatenate([v[:n], v[n:]], axis=1)


def unpacked(v):
    m = v.shape[1] // 2
    return jnp.concatenate([v[:, :m], v[:, m:]], axis=0)


def bases_kernel(new_hbm, codes_hbm, scales_hbm, new_out, old_out, new_ref, codes_ref, scales_ref, sems):
    copies = [
        pltpu.make_async_copy(source, target, sems.at[n])
        for n, (source, target) in enumerate(
            ((new_hbm, new_ref), (codes_hbm, codes_ref), (scales_hbm, scales_ref))
        )
    ]
    for copy in copies:
        copy.start()
    copies[0].wait()
    new_out[...] = packed(new_ref[...].T.astype(jnp.bfloat16))
    r = lax.axis_index("row")
    odd = lax.rem(r, 2) == 1
    first = lax.div(r * 7, 2)
    copies[1].wait()
    copies[2].wait()
    for k in range(7):
        rows = slice(k * 64, (k + 1) * 64)
        group = first + jnp.where(odd, (k + 1) // 2, k // 2)
        scale = scales_ref[pl.ds(group, 1), :]
        part = (codes_ref[rows].astype(jnp.float32) * scale).astype(jnp.bfloat16)
        if k < 3:
            old_out[rows, :B] = part
        elif k == 3:
            old_out[k * 64 :, :B] = part[:32]
            old_out[:32, B:] = part[32:]
        else:
            old_out[k * 64 - HALF : (k + 1) * 64 - HALF, B:] = part


OLD_ORDER = ((0, 0), (0, 1), (1, 0), (1, 1), (3, 0), (3, 1), (2, 0), (2, 1))


def margin_kernel(slot, a_ref, *refs):
    b_refs, outs = refs[:8], refs[8:]
    row = lax.axis_index("row")
    x = lax.div(lax.rem(row, 8), 2)
    c = lax.rem(row, 2)
    total = None
    for b_ref, (t, u) in zip(b_refs, OLD_ORDER):
        kb = lax.rem(x + t, 4) * 2 + (c if u == 0 else 1 - c)
        term = jnp.dot(
            unpacked(a_ref[kb]), unpacked(b_ref[...]), preferred_element_type=jnp.float32
        )
        total = term if total is None else total + term
    for half, out_ref in enumerate(outs):
        part = total[half * HALF : (half + 1) * HALF]
        out_ref[...] = packed(part.astype(jnp.bfloat16)) if slot == 0 else part


def margin_sum_kernel(keep_ref, other_ref, margin_ref, out_ref):
    margin = keep_ref[...] + unpacked(other_ref[...]).astype(jnp.float32)
    margin_ref[...] = margin
    out_ref[...] = packed(margin.astype(jnp.bfloat16))


def moment_kernel(moment_ref, out_ref):
    out_ref[...] = packed(moment_ref[...].astype(jnp.bfloat16))


def moment_pair_kernel(own_ref, in_ref, out_ref, relay_ref, pair_ref):
    edge = lax.div(lax.axis_index("col"), 8) == lax.div(lax.axis_index("row"), 8)
    width = pair_ref.shape[1] // 2

    @pl.when(edge)
    def _():
        pair_ref[:, :width] = unpacked(out_ref[...])
        pair_ref[:, width:] = unpacked(own_ref[...])

    @pl.when(jnp.logical_not(edge))
    def _():
        pair_ref[:, :width] = unpacked(in_ref[...])
        pair_ref[:, width:] = unpacked(relay_ref[...])


def rotate_kernel(slot, b_ref, *refs):
    a_refs, out_ref = refs[:8], refs[8]
    z = lax.rem(lax.axis_index("col"), 8)
    width = b_ref.shape[2] // 2
    total = None
    for s in range(8):
        term = jnp.dot(
            unpacked(a_refs[s][...]),
            b_ref[lax.rem(z + s, 8), :, slot * width : (slot + 1) * width],
            preferred_element_type=jnp.float32,
        )
        total = term if total is None else total + term
    out_ref[...] = packed(total.astype(jnp.bfloat16)) if slot == 0 else total


def rotate_sum_kernel(keep_a, other_a, keep_b, other_b, out_ref):
    out_ref[:HALF] = keep_a[...] + unpacked(other_a[...]).astype(jnp.float32)
    out_ref[HALF:] = keep_b[...] + unpacked(other_b[...]).astype(jnp.float32)


def z_gather(top, bottom, margin):
    rings = []
    ups, downs = ([top], [bottom]), ([top], [bottom])
    for step in range(4):
        for i in range(2):
            if step < 3 or i == 0:
                ups[i].append(send(ups[i][-1], Z_UP))
            if step < 3 or i == 1:
                downs[i].append(send(downs[i][-1], Z_DOWN))
        if step == 1:
            ups[0][-1], margin = rounds(ups[0][-1], margin)
    for i in range(2):
        u, d = ups[i], downs[i]
        far = u[4] if i == 0 else d[4]
        rings.append([u[0], d[1], d[2], d[3], far, u[3], u[2], u[1]])
    return rings, margin


def body(basis_codes, code_scales, new_basis, moment):
    width = moment.shape[1]
    bf16, f32 = jnp.bfloat16, jnp.float32
    new_t, o = call(
        bases_kernel,
        [((HALF, 2 * B), bf16)] * 2,
        [new_basis, basis_codes, code_scales],
        space=pl.ANY,
        scratch=(
            pltpu.VMEM((B, B), f32),
            pltpu.VMEM((B, B), bf16),
            pltpu.VMEM(code_scales.shape, f32),
            pltpu.SemaphoreType.DMA((3,)),
        ),
        grant=60,
    )
    groups8 = [list(range(8)), list(range(8, 16))]
    a_all = lax.all_gather(new_t, "col", axis_index_groups=groups8)
    edge = lax.axis_index("col") // 8 == lax.axis_index("row") // 8

    o_in, o_out = send(o, Y_SWAP), send(o, Y_OUT)
    o_in, o_out, moment = rounds(o_in, o_out, moment)
    o0 = jnp.where(edge, o_out, o_in)
    o_relay, o0b, o0a = send(o_in, Y_RELAY), send(o0, X_UP), send(o0, X_DOWN)
    (m,) = call(moment_kernel, [((HALF, 2 * width), bf16)], [moment])
    m_in, m_out = send(m, Y_SWAP), send(m, Y_OUT)
    o_relay, o0b, o0a = rounds(o_relay, o0b, o0a)
    o1 = jnp.where(edge, o, o_relay)
    o1b, o1a = send(o1, X_UP), send(o1, X_DOWN)
    m_in, o0a_, o0b_ = rounds(m_in, o0a, o0b)
    m_out, o0a_, o0b_ = rounds(m_out, o0a_, o0b_)
    o0ac, o0bc, m_relay = send(o0a_, CORE), send(o0b_, CORE), send(m_in, Y_RELAY)
    o1b, o1a, o0b, o0, o0ac, o0bc = rounds(o1b, o1a, o0b, o0, o0ac, o0bc)
    o0f, o1f = send(o0b, X_UP), send(o1a, X_DOWN)
    o0c = send(o0, CORE)
    (m01,) = call(moment_pair_kernel, [((B, 2 * width), bf16)], [m, m_in, m_out, m_relay])
    o0f, o1f, o0c, m01 = rounds(o0f, o1f, o0c, m01)
    m_all = lax.all_gather(m01, "row", axis_index_groups=groups8)
    o0f, o1f, a_all = rounds(o0f, o1f, a_all)
    o0fc, o1fc = send(o0f, CORE), send(o1f, CORE)
    o0fc, *near_1 = rounds(o0fc, o1, o1a, o1b)
    o1c, o1ac, o1bc = (send(v, CORE) for v in near_1)

    others = call(
        functools.partial(margin_kernel, 0),
        [((QUARTER, 2 * B), bf16)] * 2,
        [a_all, o0, o0c, o0a, o0ac, o0b, o0bc, o0f, o0fc],
        flops=2 * B * B * 8 * B,
    )
    keeps = call(
        functools.partial(margin_kernel, 1),
        [((HALF, B), f32)] * 2,
        [a_all, o1, o1c, o1a, o1ac, o1b, o1bc, o1f, o1fc],
        flops=2 * B * B * 8 * B,
    )
    margins, halves = [], []
    for keep, other in zip(keeps, others):
        margin, half = call(
            margin_sum_kernel,
            [((HALF, B), f32), ((QUARTER, 2 * B), bf16)],
            [keep, send(other, YL)],
        )
        margins.append(margin)
        halves.append(half)
    margin = jnp.stack(margins).reshape(B, B)
    rings, margin = z_gather(*halves, margin)
    parts = []
    for slot in range(2):
        for half, ring in enumerate(rings):
            shape = ((QUARTER, 2 * width), bf16) if slot == 0 else ((HALF, width), f32)
            (out,) = call(
                functools.partial(rotate_kernel, slot),
                [shape],
                [m_all, *ring],
                flops=2 * HALF * B * 8 * width,
            )
            parts.append(send(out, YL) if slot == 0 else out)
    other_a, other_b, keep_a, keep_b = parts
    (rotated,) = call(
        rotate_sum_kernel, [((B, width), f32)], [keep_a, other_a, keep_b, other_b]
    )
    return margin, rotated


def solution(mesh):
    return jax.shard_map(
        body,
        mesh=mesh,
        in_specs=(P("row", "col"), P(None, "col"), P("col", "row"), P("row", "col")),
        out_specs=(P("row", "col"), P("row", "col")),
        check_vma=False,
    )
```

```python
import functools

import jax
import jax.numpy as jnp
from jax import lax
from jax.experimental import pallas as pl
from jax.experimental.pallas import tpu as pltpu
from jax.sharding import PartitionSpec as P

AXES = ("row", "col")
B = 448
HALF = B // 2
QUARTER = B // 4


def dev(x, yh, yl, z, c):
    return (yh * 8 + x * 2 + c) * 16 + yl * 8 + z


def everyone():
    return [
        (x, yh, yl, z, c)
        for x in range(4)
        for yh in range(2)
        for yl in range(2)
        for z in range(8)
        for c in range(2)
    ]


def perm_of(move):
    return [(dev(*d), dev(*move(*d))) for d in everyone()]


Z_UP = perm_of(lambda x, yh, yl, z, c: (x, yh, yl, (z + 1) % 8, c))
Z_DOWN = perm_of(lambda x, yh, yl, z, c: (x, yh, yl, (z - 1) % 8, c))
X_UP = perm_of(lambda x, yh, yl, z, c: ((x + 1) % 4, yh, yl, z, c))
X_DOWN = perm_of(lambda x, yh, yl, z, c: ((x - 1) % 4, yh, yl, z, c))
CORE = perm_of(lambda x, yh, yl, z, c: (x, yh, yl, z, 1 - c))
YL = perm_of(lambda x, yh, yl, z, c: (x, yh, 1 - yl, z, c))
Y_SWAP_TO = {0: 3, 3: 0, 1: 2, 2: 1}
Y_OUT_TO = {1: 0, 2: 3, 0: 1, 3: 2}


def y_perm(to, senders):
    def move(x, yh, yl, z, c):
        y = to[yh * 2 + yl]
        return (x, y // 2, y % 2, z, c)

    return [
        (dev(*d), dev(*move(*d))) for d in everyone() if d[1] * 2 + d[2] in senders
    ]


Y_SWAP = y_perm(Y_SWAP_TO, (0, 1, 2, 3))
Y_OUT = y_perm(Y_OUT_TO, (1, 2))
Y_RELAY = y_perm(Y_OUT_TO, (0, 3))
Y_BOTH = y_perm(Y_OUT_TO, (0, 1, 2, 3))


def send(v, perm):
    return lax.ppermute(v, AXES, perm)


def rounds(*values):
    return lax.optimization_barrier(values)


def call(kernel, shapes, operands, flops=0, space=pltpu.VMEM, scratch=(), grant=12):
    shapes = [jax.ShapeDtypeStruct(shape, kind) for shape, kind in shapes]
    moved = sum(v.size * v.dtype.itemsize for v in [*operands, *shapes])
    return pl.pallas_call(
        kernel,
        out_shape=shapes,
        in_specs=[pl.BlockSpec(memory_space=space)] * len(operands),
        out_specs=[pl.BlockSpec(memory_space=pltpu.VMEM)] * len(shapes),
        scratch_shapes=scratch,
        compiler_params=pltpu.CompilerParams(vmem_limit_bytes=grant * 1024 * 1024),
        cost_estimate=pl.CostEstimate(
            flops=flops, bytes_accessed=moved, transcendentals=0
        ),
    )(*operands)


def packed(v):
    n = v.shape[0] // 2
    return jnp.concatenate([v[:n], v[n:]], axis=1)


def unpacked(v):
    m = v.shape[1] // 2
    return jnp.concatenate([v[:, :m], v[:, m:]], axis=0)


def bases_kernel(new_hbm, codes_hbm, scales_hbm, new_out, old_out, new_ref, codes_ref, scales_ref, sems):
    copies = [
        pltpu.make_async_copy(source, target, sems.at[n])
        for n, (source, target) in enumerate(
            ((new_hbm, new_ref), (codes_hbm, codes_ref), (scales_hbm, scales_ref))
        )
    ]
    for copy in copies:
        copy.start()
    copies[0].wait()
    new_out[...] = packed(new_ref[...].T.astype(jnp.bfloat16))
    r = lax.axis_index("row")
    odd = lax.rem(r, 2) == 1
    first = lax.div(r * 7, 2)
    copies[1].wait()
    copies[2].wait()
    for k in range(7):
        rows = slice(k * 64, (k + 1) * 64)
        group = first + jnp.where(odd, (k + 1) // 2, k // 2)
        scale = scales_ref[pl.ds(group, 1), :]
        part = (codes_ref[rows].astype(jnp.float32) * scale).astype(jnp.bfloat16)
        if k < 3:
            old_out[rows, :B] = part
        elif k == 3:
            old_out[k * 64 :, :B] = part[:32]
            old_out[:32, B:] = part[32:]
        else:
            old_out[k * 64 - HALF : (k + 1) * 64 - HALF, B:] = part


OLD_ORDER = ((0, 0), (0, 1), (1, 0), (1, 1), (3, 0), (3, 1), (2, 0), (2, 1))


def margin_kernel(slot, a_ref, *refs):
    b_refs, outs = refs[:8], refs[8:]
    row = lax.axis_index("row")
    x = lax.div(lax.rem(row, 8), 2)
    c = lax.rem(row, 2)
    total = None
    for b_ref, (t, u) in zip(b_refs, OLD_ORDER):
        kb = lax.rem(x + t, 4) * 2 + (c if u == 0 else 1 - c)
        term = jnp.dot(
            unpacked(a_ref[kb]), unpacked(b_ref[...]), preferred_element_type=jnp.float32
        )
        total = term if total is None else total + term
    for half, out_ref in enumerate(outs):
        part = total[half * HALF : (half + 1) * HALF]
        out_ref[...] = packed(part.astype(jnp.bfloat16)) if slot == 0 else part


def margin_sum_kernel(keep_ref, other_ref, margin_ref, out_ref):
    margin = keep_ref[...] + unpacked(other_ref[...]).astype(jnp.float32)
    margin_ref[...] = margin
    out_ref[...] = packed(margin.astype(jnp.bfloat16))


def moment_kernel(moment_ref, out_ref):
    out_ref[...] = packed(moment_ref[...].astype(jnp.bfloat16))


def moment_pair_kernel(own_ref, in_ref, out_ref, pair_ref):
    edge = lax.div(lax.axis_index("col"), 8) == lax.div(lax.axis_index("row"), 8)
    width = pair_ref.shape[1] // 2

    @pl.when(edge)
    def _():
        pair_ref[:, :width] = unpacked(out_ref[...])
        pair_ref[:, width:] = unpacked(own_ref[...])

    @pl.when(jnp.logical_not(edge))
    def _():
        pair_ref[:, :width] = unpacked(in_ref[...])
        pair_ref[:, width:] = unpacked(out_ref[...])


def rotate_kernel(slot, b_ref, *refs):
    a_refs, out_ref = refs[:8], refs[8]
    z = lax.rem(lax.axis_index("col"), 8)
    width = b_ref.shape[2] // 2
    total = None
    for s in range(8):
        term = jnp.dot(
            unpacked(a_refs[s][...]),
            b_ref[lax.rem(z + s, 8), :, slot * width : (slot + 1) * width],
            preferred_element_type=jnp.float32,
        )
        total = term if total is None else total + term
    out_ref[...] = packed(total.astype(jnp.bfloat16)) if slot == 0 else total


def rotate_sum_kernel(keep_a, other_a, keep_b, other_b, out_ref):
    out_ref[:HALF] = keep_a[...] + unpacked(other_a[...]).astype(jnp.float32)
    out_ref[HALF:] = keep_b[...] + unpacked(other_b[...]).astype(jnp.float32)


def z_gather(top, bottom, margin):
    rings = []
    ups, downs = ([top], [bottom]), ([top], [bottom])
    for step in range(4):
        for i in range(2):
            if step < 3 or i == 0:
                ups[i].append(send(ups[i][-1], Z_UP))
            if step < 3 or i == 1:
                downs[i].append(send(downs[i][-1], Z_DOWN))
        if step == 1:
            ups[0][-1], margin = rounds(ups[0][-1], margin)
    for i in range(2):
        u, d = ups[i], downs[i]
        far = u[4] if i == 0 else d[4]
        rings.append([u[0], d[1], d[2], d[3], far, u[3], u[2], u[1]])
    return rings, margin


def body(basis_codes, code_scales, new_basis, moment):
    width = moment.shape[1]
    bf16, f32 = jnp.bfloat16, jnp.float32
    new_t, o = call(
        bases_kernel,
        [((HALF, 2 * B), bf16)] * 2,
        [new_basis, basis_codes, code_scales],
        space=pl.ANY,
        scratch=(
            pltpu.VMEM((B, B), f32),
            pltpu.VMEM((B, B), bf16),
            pltpu.VMEM(code_scales.shape, f32),
            pltpu.SemaphoreType.DMA((3,)),
        ),
        grant=60,
    )
    groups8 = [list(range(8)), list(range(8, 16))]
    a_all = lax.all_gather(new_t, "col", axis_index_groups=groups8)
    edge = lax.axis_index("col") // 8 == lax.axis_index("row") // 8

    o_in, o_out = send(o, Y_SWAP), send(o, Y_OUT)
    o_in, o_out, moment = rounds(o_in, o_out, moment)
    o0 = jnp.where(edge, o_out, o_in)
    o_relay, o0b, o0a = send(o_in, Y_RELAY), send(o0, X_UP), send(o0, X_DOWN)
    (m,) = call(moment_kernel, [((HALF, 2 * width), bf16)], [moment])
    m_in = send(m, Y_SWAP)
    o_relay, o0b, o0a = rounds(o_relay, o0b, o0a)
    o1 = jnp.where(edge, o, o_relay)
    o1b, o1a = send(o1, X_UP), send(o1, X_DOWN)
    m_in, o0a_, o0b_ = rounds(m_in, o0a, o0b)
    m_out = send(jnp.where(edge, m_in, m), Y_BOTH)
    o0ac, o0bc = send(o0a_, CORE), send(o0b_, CORE)
    o1b, o1a, o0b, o0, o0ac, o0bc = rounds(o1b, o1a, o0b, o0, o0ac, o0bc)
    o0f, o1f = send(o0b, X_UP), send(o1a, X_DOWN)
    o0c = send(o0, CORE)
    (m01,) = call(moment_pair_kernel, [((B, 2 * width), bf16)], [m, m_in, m_out])
    o0f, o1f, o0c, m01 = rounds(o0f, o1f, o0c, m01)
    m_all = lax.all_gather(m01, "row", axis_index_groups=groups8)
    o0f, o1f, a_all = rounds(o0f, o1f, a_all)
    o0fc, o1fc = send(o0f, CORE), send(o1f, CORE)
    o0fc, *near_1 = rounds(o0fc, o1, o1a, o1b)
    o1c, o1ac, o1bc = (send(v, CORE) for v in near_1)

    others = call(
        functools.partial(margin_kernel, 0),
        [((QUARTER, 2 * B), bf16)] * 2,
        [a_all, o0, o0c, o0a, o0ac, o0b, o0bc, o0f, o0fc],
        flops=2 * B * B * 8 * B,
    )
    keeps = call(
        functools.partial(margin_kernel, 1),
        [((HALF, B), f32)] * 2,
        [a_all, o1, o1c, o1a, o1ac, o1b, o1bc, o1f, o1fc],
        flops=2 * B * B * 8 * B,
    )
    margins, halves = [], []
    for keep, other in zip(keeps, others):
        margin, half = call(
            margin_sum_kernel,
            [((HALF, B), f32), ((QUARTER, 2 * B), bf16)],
            [keep, send(other, YL)],
        )
        margins.append(margin)
        halves.append(half)
    margin = jnp.stack(margins).reshape(B, B)
    rings, margin = z_gather(*halves, margin)
    parts = []
    for slot in range(2):
        for half, ring in enumerate(rings):
            shape = ((QUARTER, 2 * width), bf16) if slot == 0 else ((HALF, width), f32)
            (out,) = call(
                functools.partial(rotate_kernel, slot),
                [shape],
                [m_all, *ring],
                flops=2 * HALF * B * 8 * width,
            )
            parts.append(send(out, YL) if slot == 0 else out)
    other_a, other_b, keep_a, keep_b = parts
    (rotated,) = call(
        rotate_sum_kernel, [((B, width), f32)], [keep_a, other_a, keep_b, other_b]
    )
    return margin, rotated


def solution(mesh):
    return jax.shard_map(
        body,
        mesh=mesh,
        in_specs=(P("row", "col"), P(None, "col"), P("col", "row"), P("row", "col")),
        out_specs=(P("row", "col"), P("row", "col")),
        check_vma=False,
    )
```
